32 devices in a mesh: ctx: 8 (over z, x), own: 4 (over y, core).
Axes of the slice: x: 2, y: 2, z: 4, core: 2. Of those that a mesh axis runs over, the one named last changes fastest.
Arguments:
- query_proj: bfloat16 [4096, 8192], P(('ctx', 'own')), may hold values from -6 to 6
- key_proj: bfloat16 [4096, 8192], P(('ctx', 'own')), may hold values from -6 to 6
- value_proj: bfloat16 [4096, 8192], P(('ctx', 'own')), may hold values from -6 to 6
- short_taps: float32 [3, 7, 512], P(None, None, 'own'), may hold values from -2 to 2
- long_taps: float32 [128, 512], P(None, 'own'), may hold values from -0.5 to 0.5
- decay_rate: float32 [8, 8192], P(None, 'own'), may hold values from 1.2207031e-05 to 0.03
- residues: float32 [8, 8192], P(None, 'own'), may hold values from -2 to 2
- grad_out: bfloat16 [4096, 8192], P(('ctx', 'own')), may hold values from -6 to 6
Outputs:
- layer_out: bfloat16 [4096, 8192], P(('ctx', 'own'))
- grad_query: bfloat16 [4096, 8192], P(('ctx', 'own'))
- grad_key: bfloat16 [4096, 8192], P(('ctx', 'own'))
- grad_value: bfloat16 [4096, 8192], P(('ctx', 'own'))
- grad_long_taps: float32 [128, 512], P(None, 'own')
The draws below stay inside these ranges and needn't reach their ends.
All inputs are finite; a program needn't handle non-finite values.
Results may differ from the reference program's by a relative error of at most 0.02.
Values may be sent and summed in bfloat16 or wider, within the bound.
A program may use at most 256 MiB of HBM per device.

```python
import math
import jax
import jax.numpy as jnp
from jax import lax

D = 8192
ORDER = 8
SHORT = 7
TAPS = 128
CPG = 16
G = 512
TOKENS = 4096


def shard_levels(key, shape, shards, low, top_value):
    def one(position, parts):
        heights = jax.random.uniform(jax.random.fold_in(jax.random.fold_in(key, 6), position), (parts,), jnp.float32, low / len(shards), top_value / len(shards))
        return jnp.repeat(jnp.exp(heights), shape[position] // parts).reshape((-1,) + (1,) * (len(shape) - position - 1))

    level = one(*shards[0])
    for cut in shards[1:]:
        level = level * one(*cut)
    return level


def bell_draw(stream_key, dims, spread, most, split=(), held_as=jnp.bfloat16):
    result = spread * jax.random.normal(stream_key, dims, jnp.float32)
    if split:
        result = result * shard_levels(stream_key, dims, split, -0.22, 0.18)
    return jnp.clip(result, -most, most).astype(held_as)


def setup_inputs(seed: int = 0) -> dict:
    seeds = jax.random.split(jax.random.key(seed), 9)
    return {
        "query_proj": bell_draw(seeds[0], (TOKENS, D), 1.0, 6.0, ((0, 32),)),
        "key_proj": bell_draw(seeds[1], (TOKENS, D), 1.0, 6.0, ((0, 32),)),
        "value_proj": bell_draw(seeds[2], (TOKENS, D), 1.0, 6.0, ((0, 32),)),
        "short_taps": bell_draw(seeds[3], (3, SHORT, G), SHORT ** -0.5, 2.0, ((2, 4),), jnp.float32),
        "long_taps": bell_draw(seeds[4], (TAPS, G), TAPS ** -0.5, 0.5, ((1, 4),), jnp.float32),
        "decay_rate": jnp.clip(jnp.exp(math.log(0.03) - 7.8069405 * jax.random.uniform(seeds[5], (ORDER, D), jnp.float32) ** shard_levels(seeds[5], (ORDER, D), ((1, 4),), -0.2, 0.2)), 1.220703143189894e-05, 0.03),
        "residues": bell_draw(seeds[6], (ORDER, D), ORDER ** -0.5, 2.0, ((1, 4),), jnp.float32),
        "grad_out": bell_draw(seeds[7], (TOKENS, D), 1.0, 6.0, ((0, 32),)),
    }


def causal_short(rows_in, taps_chan):
    values = rows_in.astype(jnp.float32)
    row_count, chan_count = values.shape
    summed = jnp.zeros((row_count, chan_count), jnp.float32)
    for offset in range(SHORT):
        moved = jnp.concatenate([jnp.zeros((offset, chan_count), jnp.float32), values[:row_count - offset]], axis=0)
        summed = summed + taps_chan[offset][None, :] * moved
    return summed.astype(jnp.bfloat16)

def later_short(rows_in, taps_chan):
    values = rows_in.astype(jnp.float32)
    row_count, chan_count = values.shape
    summed = jnp.zeros((row_count, chan_count), jnp.float32)
    for offset in range(SHORT):
        moved = jnp.concatenate([values[offset:], jnp.zeros((offset, chan_count), jnp.float32)], axis=0)
        summed = summed + taps_chan[offset][None, :] * moved
    return summed.astype(jnp.bfloat16)

def one_block(query, key_rows, value_rows, grad_rows, short_part, taps_part, decay, resid):
    chan_short = jnp.repeat(short_part, CPG, axis=2)
    query_feat = causal_short(query, chan_short[0])
    key_feat = causal_short(key_rows, chan_short[1])
    value_feat = causal_short(value_rows, chan_short[2])
    product = (key_feat.astype(jnp.float32) * value_feat.astype(jnp.float32)).astype(jnp.bfloat16)
    positions = jnp.arange(TOKENS).astype(jnp.float32)
    weight = resid * jnp.sqrt(-jnp.expm1(-2.0 * decay))

    def add_mode(summed, mode):
        return (summed + mode[0][None, :] * jnp.exp(-mode[1][None, :] * positions[:, None]), None)
    start_value = jnp.zeros((TOKENS, decay.shape[1]), jnp.float32)
    filter_full, _ = lax.scan(add_mode, start_value, (weight, decay))
    filter_full = filter_full + jnp.pad(jnp.repeat(taps_part, CPG, axis=1), ((0, TOKENS - TAPS), (0, 0)))
    fft_size = 2 * TOKENS
    filter_spec = jnp.fft.rfft(filter_full, n=fft_size, axis=0)
    product_spec = jnp.fft.rfft(product.astype(jnp.float32), n=fft_size, axis=0)
    long_conv = jnp.fft.irfft(product_spec * filter_spec, n=fft_size, axis=0)[:TOKENS]
    grad_float = grad_rows.astype(jnp.float32)
    layer_out = (query_feat.astype(jnp.float32) * long_conv).astype(jnp.bfloat16)
    grad_conv = (grad_float * query_feat.astype(jnp.float32)).astype(jnp.bfloat16)
    grad_qfeat = (grad_float * long_conv).astype(jnp.bfloat16)
    conv_spec = jnp.fft.rfft(grad_conv.astype(jnp.float32), n=fft_size, axis=0)
    grad_prod = jnp.fft.irfft(conv_spec * jnp.conj(filter_spec), n=fft_size, axis=0)[:TOKENS]
    grad_kfeat = (grad_prod * value_feat.astype(jnp.float32)).astype(jnp.bfloat16)
    grad_vfeat = (grad_prod * key_feat.astype(jnp.float32)).astype(jnp.bfloat16)
    grad_query = later_short(grad_qfeat, chan_short[0])
    grad_key = later_short(grad_kfeat, chan_short[1])
    grad_value = later_short(grad_vfeat, chan_short[2])
    correlation = jnp.fft.irfft(conv_spec * jnp.conj(product_spec), n=fft_size, axis=0)[:TAPS]
    group_count = correlation.shape[1] // CPG
    grad_taps = correlation.reshape(TAPS, group_count, CPG).sum(axis=2) / math.sqrt(TOKENS * CPG)
    return (layer_out, grad_query, grad_key, grad_value, grad_taps)

def reference(query_proj, key_proj, value_proj, short_taps, long_taps, decay_rate, residues, grad_out):
    groups = D // CPG
    block_groups = math.gcd(groups, 16)
    block_chan = block_groups * CPG

    def one_step(block_index, outputs):
        first_chan = (block_index * block_chan).astype(jnp.int32)
        first_group = (block_index * block_groups).astype(jnp.int32)

        def chan_slice(array):
            return lax.dynamic_slice_in_dim(array, first_chan, block_chan, array.ndim - 1)

        def group_slice(array):
            return lax.dynamic_slice_in_dim(array, first_group, block_groups, array.ndim - 1)
        results = one_block(chan_slice(query_proj), chan_slice(key_proj), chan_slice(value_proj), chan_slice(grad_out), group_slice(short_taps), group_slice(long_taps), chan_slice(decay_rate), chan_slice(residues))
        updated = []
        for position_out in range(4):
            updated.append(lax.dynamic_update_slice_in_dim(outputs[position_out], results[position_out], first_chan, 1))
        updated.append(lax.dynamic_update_slice_in_dim(outputs[4], results[4], first_group, 1))
        return tuple(updated)
    initial = (jnp.zeros((TOKENS, D), jnp.bfloat16), jnp.zeros((TOKENS, D), jnp.bfloat16), jnp.zeros((TOKENS, D), jnp.bfloat16), jnp.zeros((TOKENS, D), jnp.bfloat16), jnp.zeros((TAPS, groups), jnp.float32))
    layer_out, grad_query, grad_key, grad_value, grad_taps = lax.fori_loop(0, groups // block_groups, one_step, initial)
    return (layer_out, grad_query, grad_key, grad_value, grad_taps)
```

```python
import functools
import math

import jax
import jax.numpy as jnp
from jax import lax
from jax.experimental import pallas as pl
from jax.experimental.pallas import tpu as pltpu
from jax.sharding import PartitionSpec as P

AXES = ("ctx", "own")
SUB = 8
f32, bf16 = jnp.float32, jnp.bfloat16
VMEM_LIMIT = 48 * 1024 * 1024


def from_behind(value, axis, steps):
    count = lax.axis_size(axis)
    leading, last = (max(0, -steps), min(count, count - steps))
    return lax.ppermute(value, axis, [(source, source + steps) for source in range(leading, last)])


def mm(a, b):
    return jnp.dot(a, b, preferred_element_type=f32)


def odd_tables(rows):
    odd = 2 * jnp.arange(rows, dtype=jnp.int32)[:, None] + 1
    place = jnp.arange(rows, dtype=jnp.int32)[None, :]

    def matrix(at):
        angle = ((odd * at) % (4 * rows)).astype(f32) * (math.pi / (2 * rows))
        return jnp.concatenate([jnp.cos(angle), -jnp.sin(angle)], axis=0)

    here, before = matrix(place), matrix(place + 3 * rows)
    back = here.T / rows
    return here.astype(bf16), before.astype(bf16), back.astype(bf16)


def spread_matrix(groups, width, cpg, first):
    row = lax.broadcasted_iota(jnp.int32, (groups, width), 0)
    col = lax.broadcasted_iota(jnp.int32, (groups, width), 1)
    start = (row - first) * cpg
    return jnp.logical_and(col >= start, col < start + cpg)


def conv_rows(rim, main, taps):
    rows = main.shape[0]
    joined = jnp.concatenate([rim, main], axis=0)
    total = taps[0:1] * main
    for j in range(1, taps.shape[0]):
        total = total + taps[j : j + 1] * pltpu.roll(joined, j, 0)[SUB:]
    return total


def corr_rows(main, rim, taps):
    rows = main.shape[0]
    joined = jnp.concatenate([main, rim], axis=0)
    total = taps[0:1] * main
    for j in range(1, taps.shape[0]):
        total = total + taps[j : j + 1] * pltpu.roll(joined, rows + SUB - j, 0)[:rows]
    return total


def modal_rows(coeff, decay, rows, reverse):
    poles, width = decay.shape
    step = lax.broadcasted_iota(jnp.int32, (SUB, width), 0).astype(f32)
    lag = (SUB - step) if reverse else step
    hop = jnp.exp(-float(SUB) * decay)
    now = [coeff[r : r + 1] * jnp.exp(-decay[r : r + 1] * lag) for r in range(poles)]
    hops = [jnp.broadcast_to(hop[r : r + 1], (SUB, width)) for r in range(poles)]
    parts = []
    for k in range(rows // SUB):
        total = now[0]
        for r in range(1, poles):
            total = total + now[r]
        parts.append(total)
        if k + 1 < rows // SUB:
            now = [a * b for a, b in zip(now, hops)]
    if reverse:
        parts = parts[::-1]
    return jnp.concatenate(parts, axis=0)


def block_states(x, decay, reverse):
    poles, width = decay.shape
    rows = x.shape[0]
    step = lax.broadcasted_iota(jnp.int32, (SUB, width), 0).astype(f32)
    lag = step if reverse else (SUB - 1 - step)
    hop = jnp.exp(-float(SUB) * decay)
    order = list(range(rows // SUB))
    if reverse:
        order = order[::-1]
    states = []
    for r in range(poles):
        one = jnp.broadcast_to(hop[r : r + 1], (SUB, width))
        total = x[order[0] * SUB : (order[0] + 1) * SUB]
        for k in order[1:]:
            total = total * one + x[k * SUB : (k + 1) * SUB]
        states.append(
            jnp.sum(total * jnp.exp(-decay[r : r + 1] * lag), axis=0, keepdims=True)
        )
    return jnp.concatenate(states, axis=0)


def pieces(tile, width, body):
    def step(i, carry):
        body(i, pl.ds(pl.multiple_of(i * width, width), width))
        return carry

    lax.fori_loop(0, tile // width, step, 0)


def short_of(short_ref, groups, width, cpg, i):
    spread = spread_matrix(groups, width, cpg, i * (width // cpg)).astype(f32)
    return jnp.dot(
        short_ref[...], spread, precision=lax.Precision.HIGHEST, preferred_element_type=f32
    )


def first_kernel(
    cpg, width, taps, q_ref, k_ref, v_ref, g_ref, rim_ref, short_ref, decay_ref,
    qf_ref, kf_ref, vf_ref, p_ref, gc_ref, st_ref,
):
    groups = short_ref.shape[1]

    def body(i, at):
        short = short_of(short_ref, groups, width, cpg, i)
        rim = rim_ref[:, at].astype(f32)

        def feat(n, ref):
            out = conv_rows(
                rim[n * SUB : (n + 1) * SUB],
                ref[:, at].astype(f32),
                short[n * SUB : n * SUB + taps],
            )
            return out.astype(bf16)

        qf, kf, vf = feat(0, q_ref), feat(1, k_ref), feat(2, v_ref)
        qf_ref[:, at] = qf
        kf_ref[:, at] = kf
        vf_ref[:, at] = vf
        product = (kf.astype(f32) * vf.astype(f32)).astype(bf16)
        p_ref[:, at] = product
        conv = (g_ref[:, at].astype(f32) * qf.astype(f32)).astype(bf16)
        gc_ref[:, at] = conv
        decay = decay_ref[:, at]
        poles = decay.shape[0]
        st_ref[:, at] = jnp.concatenate(
            [
                block_states(product.astype(f32), decay, False),
                block_states(conv.astype(f32), decay, True),
            ],
            axis=0,
        ).astype(bf16)

    pieces(q_ref.shape[1], width, body)


def times(a, b, rows):
    ar, ai, br, bi = a[:rows], a[rows:], b[:rows], b[rows:]
    return jnp.concatenate([ar * br - ai * bi, ar * bi + ai * br], axis=0).astype(bf16)


def times_conj(a, b, rows):
    ar, ai, br, bi = a[:rows], a[rows:], b[:rows], b[rows:]
    return jnp.concatenate([ar * br + ai * bi, ai * br - ar * bi], axis=0).astype(bf16)


def group_total(spec, groups, width, cpg, i):
    spread = spread_matrix(groups, width, cpg, i * (width // cpg)).astype(bf16)
    return lax.dot_general(
        spec, spread, (((1,), (1,)), ((), ())), preferred_element_type=f32
    )


def own_kernel(
    cpg, width, here_ref, back_ref, p_ref, gc_ref, decay_ref, weight_ref, long_ref,
    near_ref, nearb_ref, taps_ref, corr_ref,
):
    rows, tile = p_ref.shape
    groups = long_ref.shape[1]
    corr_ref[...] = jnp.zeros_like(corr_ref)

    def body(i, at):
        spread = spread_matrix(groups, width, cpg, i * (width // cpg)).astype(bf16)
        head = modal_rows(weight_ref[:, at], decay_ref[:, at], rows, False)
        head = head + mm(long_ref[...].astype(bf16), spread)
        head_spec = mm(here_ref[...], head.astype(bf16))
        own = mm(here_ref[...], p_ref[:, at])
        cur = mm(here_ref[...], gc_ref[:, at])
        near_ref[:, at] = mm(back_ref[...], times(own, head_spec, rows)).astype(bf16)
        nearb_ref[:, at] = mm(back_ref[...], times_conj(cur, head_spec, rows)).astype(bf16)
        corr_ref[...] += group_total(times_conj(cur, own, rows), groups, width, cpg, i)

    pieces(tile, width, body)
    taps_ref[...] = mm(back_ref[...], corr_ref[...].astype(bf16))


def last_kernel(
    cpg, width, taps, scale, here_ref, before_ref, back_ref, prev_ref, next_ref, gc_ref,
    near_ref, nearb_ref, qf_ref, kf_ref, vf_ref, g_ref, state_ref, decay_ref, weight_ref,
    long_ref, short_ref, tapsin_ref,
    lay_ref, gq_ref, gk_ref, gv_ref, head_ref, tail_ref, taps_ref, corr_ref, edge_ref,
):
    rows, tile = prev_ref.shape
    groups = long_ref.shape[1]
    corr_ref[...] = jnp.zeros_like(corr_ref)
    edge_ref[...] = mm(here_ref[...], long_ref[...].astype(bf16)).astype(bf16)

    def body(i, at):
        spread = spread_matrix(groups, width, cpg, i * (width // cpg)).astype(bf16)
        short = short_of(short_ref, groups, width, cpg, i)
        edge = mm(edge_ref[...], spread)
        prev = mm(before_ref[...], prev_ref[:, at])
        nxt = -mm(before_ref[...], next_ref[:, at])
        cur = mm(here_ref[...], gc_ref[:, at])
        decay, weight = decay_ref[:, at], weight_ref[:, at]
        poles = decay.shape[0]
        state = state_ref[:, at].astype(f32)
        corr_ref[...] += group_total(times_conj(cur, prev, rows), groups, width, cpg, i)
        conv = near_ref[:, at].astype(f32) + mm(back_ref[...], times(prev, edge, rows))
        conv = conv + modal_rows(
            weight * jnp.exp(-decay) * state[:poles], decay, rows, False
        )
        lay_ref[:, at] = (qf_ref[:, at].astype(f32) * conv).astype(bf16)
        grad = nearb_ref[:, at].astype(f32) + mm(back_ref[...], times_conj(nxt, edge, rows))
        grad = grad + modal_rows(weight * state[poles:], decay, rows, True)
        zero = jnp.zeros((SUB, width), f32)

        def finish(n, value, out_ref):
            value = value.astype(bf16)
            head_ref[n * SUB : (n + 1) * SUB, at] = value[:SUB]
            out = corr_rows(value.astype(f32), zero, short[n * SUB : n * SUB + taps])
            tail_ref[n * SUB : (n + 1) * SUB, at] = out[rows - SUB :]
            out_ref[:, at] = out.astype(bf16)

        finish(0, g_ref[:, at].astype(f32) * conv, gq_ref)
        finish(1, grad * vf_ref[:, at].astype(f32), gk_ref)
        finish(2, grad * kf_ref[:, at].astype(f32), gv_ref)

    pieces(tile, width, body)
    total = tapsin_ref[...] + mm(back_ref[...], corr_ref[...].astype(bf16))
    taps_ref[...] = (total * scale).astype(bf16)


def edge_kernel(cpg, width, taps, rim_ref, tail_ref, short_ref, *refs):
    olds, outs = refs[:3], refs[3:]
    groups = short_ref.shape[1]

    def body(i, at):
        short = short_of(short_ref, groups, width, cpg, i)
        for n in range(3):
            part = short[n * SUB : n * SUB + taps]
            zero = jnp.zeros((SUB, width), f32)
            rim = rim_ref[n * SUB : (n + 1) * SUB, at].astype(f32)
            add = corr_rows(zero, rim, part)
            low = tail_ref[n * SUB : (n + 1) * SUB, at] + add
            outs[n][:, at] = jnp.concatenate(
                [olds[n][:SUB, at].astype(f32), low], axis=0
            ).astype(bf16)

    pieces(tail_ref.shape[1], width, body)


def scan_kernel(x_ref, rate_ref, out_ref):
    count = x_ref.shape[0]
    poles = rate_ref.shape[0]
    keep = jnp.exp(-rate_ref[...])

    def step(k, carry):
        ahead, behind = carry
        out_ref[k, :poles] = ahead
        at = count - 1 - k
        out_ref[at, poles:] = behind
        return (
            keep * ahead + x_ref[k, :poles],
            keep * behind + x_ref[at, poles:],
        )

    zero = jnp.zeros(keep.shape, f32)
    lax.fori_loop(0, count, step, (zero, zero))


def params():
    return pltpu.CompilerParams(vmem_limit_bytes=VMEM_LIMIT)


def shards(query_proj, key_proj, value_proj, short_taps, long_taps, decay_rate, residues, grad_out):
    rows, chans = query_proj.shape
    owners = lax.axis_size("own")
    count = owners * lax.axis_size("ctx")
    tap_count = short_taps.shape[1]
    groups_own = short_taps.shape[2]
    groups = groups_own * owners
    cpg = chans // groups
    poles = decay_rate.shape[0]
    tile = groups_own * cpg
    steps = chans // tile
    width = 256
    shape = jax.ShapeDtypeStruct

    rims = from_behind(
        jnp.concatenate([query_proj[-SUB:], key_proj[-SUB:], value_proj[-SUB:]], axis=0), AXES, 1
    )
    short_pad = jnp.pad(short_taps, ((0, 0), (0, SUB - tap_count), (0, 0))).reshape(
        3 * SUB, groups_own
    )
    weight_own = residues * jnp.sqrt(-jnp.expm1(-2.0 * decay_rate))
    short_all = lax.all_gather(short_pad, "own", axis=1, tiled=True)
    modal_all = lax.all_gather(
        jnp.concatenate([decay_rate, weight_own], axis=0), "own", axis=1, tiled=True
    )
    long_all = lax.all_gather(long_taps, "own", axis=1, tiled=True)
    decay_all, weight_all = modal_all[:poles], modal_all[poles:]
    here, before, back = odd_tables(rows)

    def cols(height, wide=tile):
        return pl.BlockSpec((height, wide), lambda i: (0, i))

    def whole(height, wide):
        return pl.BlockSpec((height, wide), lambda i: (0, 0))

    big = shape((rows, chans), bf16)
    qf, kf, vf, product, conv, states = pl.pallas_call(
        functools.partial(first_kernel, cpg, width, tap_count),
        grid=(steps,),
        in_specs=[cols(rows)] * 4 + [cols(3 * SUB), cols(3 * SUB, groups_own), cols(poles)],
        out_specs=[cols(rows)] * 5 + [cols(2 * poles)],
        out_shape=[big] * 5 + [shape((2 * poles, chans), bf16)],
        compiler_params=params(),
        cost_estimate=pl.CostEstimate(
            flops=100 * rows * chans, bytes_accessed=18 * rows * chans, transcendentals=0
        ),
        name="first",
    )(query_proj, key_proj, value_proj, grad_out, rims, short_all, decay_all)

    earlier = from_behind(product, AXES, 1)
    later = from_behind(conv, AXES, -1)

    part = chans // count
    sent = states.reshape(2 * poles, count, part).transpose(1, 0, 2)
    got = lax.all_to_all(sent, AXES, 0, 0, tiled=True).astype(f32)
    me = lax.axis_index("ctx") * owners + lax.axis_index("own")
    rate = lax.dynamic_slice_in_dim(decay_all, me * part, part, 1) * float(rows)
    scanned = pl.pallas_call(
        scan_kernel, out_shape=shape((count, 2 * poles, part), f32), name="scan"
    )(got, rate)
    returned = lax.all_to_all(scanned.astype(bf16), AXES, 0, 0, tiled=True)
    state_in = returned.transpose(1, 0, 2).reshape(2 * poles, chans)

    near, near_back, taps_own = pl.pallas_call(
        functools.partial(own_kernel, cpg, width),
        grid=(steps,),
        in_specs=[
            whole(2 * rows, rows), whole(rows, 2 * rows), cols(rows), cols(rows),
            cols(poles), cols(poles), cols(long_taps.shape[0], groups_own),
        ],
        out_specs=[cols(rows), cols(rows), cols(rows, groups_own)],
        out_shape=[big, big, shape((rows, groups), f32)],
        scratch_shapes=[pltpu.VMEM((2 * rows, groups_own), f32)],
        compiler_params=params(),
        cost_estimate=pl.CostEstimate(
            flops=14 * rows * rows * chans, bytes_accessed=8 * rows * chans, transcendentals=0
        ),
        name="own",
    )(here, back, product, conv, decay_all, weight_all, long_all)

    scale = 1.0 / math.sqrt(rows * count * cpg)
    layer_out, gq, gk, gv, heads, tails, taps_part = pl.pallas_call(
        functools.partial(last_kernel, cpg, width, tap_count, scale),
        grid=(steps,),
        in_specs=[whole(2 * rows, rows), whole(2 * rows, rows), whole(rows, 2 * rows)]
        + [cols(rows)] * 9
        + [
            cols(2 * poles), cols(poles), cols(poles), cols(long_taps.shape[0], groups_own),
            cols(3 * SUB, groups_own), cols(rows, groups_own),
        ],
        out_specs=[cols(rows)] * 4 + [cols(3 * SUB), cols(3 * SUB), cols(rows, groups_own)],
        out_shape=[big] * 4
        + [
            shape((3 * SUB, chans), bf16), shape((3 * SUB, chans), f32),
            shape((rows, groups), bf16),
        ],
        scratch_shapes=[
            pltpu.VMEM((2 * rows, groups_own), f32), pltpu.VMEM((2 * rows, groups_own), bf16)
        ],
        compiler_params=params(),
        cost_estimate=pl.CostEstimate(
            flops=16 * rows * rows * chans, bytes_accessed=26 * rows * chans, transcendentals=0
        ),
        name="last",
    )(
        here, before, back, earlier, later, conv, near, near_back, qf, kf, vf, grad_out,
        state_in, decay_all, weight_all, long_all, short_all, taps_own,
    )

    rim_after = from_behind(heads, AXES, -1)
    bottom = pl.BlockSpec((2 * SUB, tile), lambda i: (rows // (2 * SUB) - 1, i))
    gq, gk, gv = pl.pallas_call(
        functools.partial(edge_kernel, cpg, width, tap_count),
        grid=(steps,),
        in_specs=[cols(3 * SUB), cols(3 * SUB), cols(3 * SUB, groups_own)] + [bottom] * 3,
        out_specs=[bottom] * 3,
        out_shape=[big] * 3,
        input_output_aliases={3: 0, 4: 1, 5: 2},
        compiler_params=params(),
        name="edge",
    )(rim_after, tails, short_all, gq, gk, gv)

    owned = lax.psum_scatter(taps_part, "own", scatter_dimension=1, tiled=True)
    grad_taps = lax.psum(owned, "ctx").astype(f32)
    return (layer_out, gq, gk, gv, grad_taps)


def solution(mesh):
    block = P(AXES, None)
    return jax.shard_map(
        shards,
        mesh=mesh,
        in_specs=(
            block, block, block, P(None, None, "own"), P(None, "own"), P(None, "own"),
            P(None, "own"), block,
        ),
        out_specs=(block, block, block, block, P(None, "own")),
        check_vma=False,
    )
```

```python
import functools
import math

import jax
import jax.numpy as jnp
from jax import lax
from jax.experimental import pallas as pl
from jax.experimental.pallas import tpu as pltpu
from jax.sharding import PartitionSpec as P

AXES = ("ctx", "own")
SUB = 8
f32, bf16 = jnp.float32, jnp.bfloat16
VMEM_LIMIT = 48 * 1024 * 1024


def from_behind(value, axis, steps):
    count = lax.axis_size(axis)
    leading, last = (max(0, -steps), min(count, count - steps))
    return lax.ppermute(value, axis, [(source, source + steps) for source in range(leading, last)])


def mm(a, b):
    return jnp.dot(a, b, preferred_element_type=f32)


def odd_tables(rows):
    odd = 2 * jnp.arange(rows, dtype=jnp.int32)[:, None] + 1
    place = jnp.arange(rows, dtype=jnp.int32)[None, :]

    def matrix(at):
        angle = ((odd * at) % (4 * rows)).astype(f32) * (math.pi / (2 * rows))
        return jnp.concatenate([jnp.cos(angle), -jnp.sin(angle)], axis=0)

    here, before = matrix(place), matrix(place + 3 * rows)
    back = here.T / rows
    return here.astype(bf16), before.astype(bf16), back.astype(bf16)


def spread_matrix(groups, width, cpg, first):
    row = lax.broadcasted_iota(jnp.int32, (groups, width), 0)
    col = lax.broadcasted_iota(jnp.int32, (groups, width), 1)
    start = (row - first) * cpg
    return jnp.logical_and(col >= start, col < start + cpg)


def conv_rows(rim, main, taps):
    rows = main.shape[0]
    joined = jnp.concatenate([rim, main], axis=0)
    total = taps[0:1] * main
    for j in range(1, taps.shape[0]):
        total = total + taps[j : j + 1] * pltpu.roll(joined, j, 0)[SUB:]
    return total


def corr_rows(main, rim, taps):
    rows = main.shape[0]
    joined = jnp.concatenate([main, rim], axis=0)
    total = taps[0:1] * main
    for j in range(1, taps.shape[0]):
        total = total + taps[j : j + 1] * pltpu.roll(joined, rows + SUB - j, 0)[:rows]
    return total


def modal_rows(coeff, decay, rows, reverse):
    poles, width = decay.shape
    step = lax.broadcasted_iota(jnp.int32, (SUB, width), 0).astype(f32)
    lag = (SUB - step) if reverse else step
    hop = jnp.exp(-float(SUB) * decay)
    now = [coeff[r : r + 1] * jnp.exp(-decay[r : r + 1] * lag) for r in range(poles)]
    hops = [jnp.broadcast_to(hop[r : r + 1], (SUB, width)) for r in range(poles)]
    parts = []
    for k in range(rows // SUB):
        total = now[0]
        for r in range(1, poles):
            total = total + now[r]
        parts.append(total)
        if k + 1 < rows // SUB:
            now = [a * b for a, b in zip(now, hops)]
    if reverse:
        parts = parts[::-1]
    return jnp.concatenate(parts, axis=0)


def block_states(x, decay, reverse):
    poles, width = decay.shape
    rows = x.shape[0]
    step = lax.broadcasted_iota(jnp.int32, (SUB, width), 0).astype(f32)
    lag = step if reverse else (SUB - 1 - step)
    hop = jnp.exp(-float(SUB) * decay)
    order = list(range(rows // SUB))
    if reverse:
        order = order[::-1]
    states = []
    for r in range(poles):
        one = jnp.broadcast_to(hop[r : r + 1], (SUB, width))
        total = x[order[0] * SUB : (order[0] + 1) * SUB]
        for k in order[1:]:
            total = total * one + x[k * SUB : (k + 1) * SUB]
        states.append(
            jnp.sum(total * jnp.exp(-decay[r : r + 1] * lag), axis=0, keepdims=True)
        )
    return jnp.concatenate(states, axis=0)


def pieces(tile, width, body):
    def step(i, carry):
        body(i, pl.ds(pl.multiple_of(i * width, width), width))
        return carry

    lax.fori_loop(0, tile // width, step, 0)


def short_of(short_ref, groups, width, cpg, i):
    spread = spread_matrix(groups, width, cpg, i * (width // cpg)).astype(bf16)
    value = short_ref[...]
    count = value.shape[0]
    high = value.astype(bf16).astype(f32)
    both = mm(jnp.concatenate([high, value - high], axis=0).astype(bf16), spread)
    return both[:count] + both[count:]


def device_of(flat, owners):
    return (lax.div(flat, owners), lax.rem(flat, owners))


def put(src, dst, send, recv, device):
    return pltpu.make_async_remote_copy(
        src_ref=src,
        dst_ref=dst,
        send_sem=send,
        recv_sem=recv,
        device_id=device,
        device_id_type=pl.DeviceIdType.MESH,
    )


def loop(count, body):
    def step(k, carry):
        body(k)
        return carry

    lax.fori_loop(1, count, step, 0)


def greet(count, device):
    barrier = pltpu.get_barrier_semaphore()
    loop(
        count,
        lambda k: pl.semaphore_signal(
            barrier, inc=1, device_id=device(k), device_id_type=pl.DeviceIdType.MESH
        ),
    )
    pl.semaphore_wait(barrier, count - 1)


def gather_kernel(owners, first_ref, second_ref, first_out, second_out, send, recv):
    ctx, own = lax.axis_index("ctx"), lax.axis_index("own")

    def device(k):
        return (ctx, lax.rem(own + k, owners))

    greet(owners, device)

    def copies(k):
        return [
            put(src, dst.at[own], send.at[n, k], recv.at[n, k], device(k))
            for n, (src, dst) in enumerate(((first_ref, first_out), (second_ref, second_out)))
        ]

    loop(owners, lambda k: [c.start() for c in copies(k)] and None)
    first_out[own] = first_ref[...]
    second_out[own] = second_ref[...]
    loop(owners, lambda k: [c.wait() for c in copies(k)] and None)


def exchange_kernel(
    owners, count, st_ref, rate_ref, w_ref, l_ref, ret_ref, w_out, l_out,
    got, work, scanned, send, recv, gsend, grecv,
):
    ctx, own = lax.axis_index("ctx"), lax.axis_index("own")
    me = ctx * owners + own
    poles = rate_ref.shape[0]

    def device(k):
        return device_of(lax.rem(me + k, count), owners)

    greet(count, device)

    def out_copy(k):
        to = lax.rem(me + k, count)
        return put(st_ref.at[to], got.at[me], send.at[0, k], recv.at[0, k], device(k))

    def back_copy(k):
        to = lax.rem(me + k, count)
        return put(scanned.at[to], ret_ref.at[me], send.at[1, k], recv.at[1, k], device(k))

    def gathers(k):
        peer = (ctx, lax.rem(own + k, owners))
        return [
            put(src, dst.at[own], gsend.at[n, k], grecv.at[n, k], peer)
            for n, (src, dst) in enumerate(((w_ref, w_out), (l_ref, l_out)))
        ]

    loop(count, lambda k: out_copy(k).start())
    loop(owners, lambda k: [c.start() for c in gathers(k)] and None)
    got[me] = st_ref[me]
    w_out[own] = w_ref[...]
    l_out[own] = l_ref[...]
    loop(count, lambda k: out_copy(k).wait())
    keep = jnp.exp(-rate_ref[...])

    def step(k, carry):
        ahead, behind = carry
        at = count - 1 - k
        work[k, :poles] = ahead
        work[at, poles:] = behind
        return (
            keep * ahead + got[k].astype(f32)[:poles],
            keep * behind + got[at].astype(f32)[poles:],
        )

    zero = jnp.zeros(keep.shape, f32)
    lax.fori_loop(0, count, step, (zero, zero))
    scanned[...] = work[...].astype(bf16)
    loop(count, lambda k: back_copy(k).start())
    ret_ref[me] = scanned[me]
    loop(count, lambda k: back_copy(k).wait())
    loop(owners, lambda k: [c.wait() for c in gathers(k)] and None)


def reduce_kernel(owners, count, part_ref, out_ref, got, send, recv, asend, arecv):
    ctx, own = lax.axis_index("ctx"), lax.axis_index("own")
    me = ctx * owners + own
    ctxs = count // owners

    def device(k):
        return device_of(lax.rem(me + k, count), owners)

    greet(count, device)

    def out_copy(k):
        to = lax.rem(me + k, count)
        return put(part_ref.at[to], got.at[me], send.at[k], recv.at[k], device(k))

    def all_copy(k):
        return put(
            out_ref.at[ctx], out_ref.at[ctx], asend.at[k], arecv.at[k],
            (lax.rem(ctx + k, ctxs), own),
        )

    loop(count, lambda k: out_copy(k).start())
    got[me] = part_ref[me]
    loop(count, lambda k: out_copy(k).wait())
    out_ref[ctx] = jnp.sum(got[...], axis=0)
    loop(ctxs, lambda k: all_copy(k).start())
    loop(ctxs, lambda k: all_copy(k).wait())


def first_kernel(
    cpg, width, taps, q_ref, k_ref, v_ref, g_ref, rim_ref, short_ref, decay_ref,
    qf_ref, kf_ref, vf_ref, p_ref, gc_ref, st_ref, sc_ref,
):
    groups = short_ref.shape[1]

    def body(i, at):
        short = short_of(short_ref, groups, width, cpg, i)
        sc_ref[:, at] = short
        rim = rim_ref[:, at].astype(f32)

        def feat(n, ref):
            out = conv_rows(
                rim[n * SUB : (n + 1) * SUB],
                ref[:, at].astype(f32),
                short[n * SUB : n * SUB + taps],
            )
            return out.astype(bf16)

        qf, kf, vf = feat(0, q_ref), feat(1, k_ref), feat(2, v_ref)
        qf_ref[:, at] = qf
        kf_ref[:, at] = kf
        vf_ref[:, at] = vf
        product = (kf.astype(f32) * vf.astype(f32)).astype(bf16)
        p_ref[:, at] = product
        conv = (g_ref[:, at].astype(f32) * qf.astype(f32)).astype(bf16)
        gc_ref[:, at] = conv
        decay = decay_ref[:, at]
        poles = decay.shape[0]
        st_ref[:, at] = jnp.concatenate(
            [
                block_states(product.astype(f32), decay, False),
                block_states(conv.astype(f32), decay, True),
            ],
            axis=0,
        ).astype(bf16)

    pieces(q_ref.shape[1], width, body)


def times(a, b, rows):
    ar, ai, br, bi = a[:rows], a[rows:], b[:rows], b[rows:]
    return jnp.concatenate([ar * br - ai * bi, ar * bi + ai * br], axis=0).astype(bf16)


def times_conj(a, b, rows):
    ar, ai, br, bi = a[:rows], a[rows:], b[:rows], b[rows:]
    return jnp.concatenate([ar * br + ai * bi, ai * br - ar * bi], axis=0).astype(bf16)


def group_total(spec, groups, width, cpg, i):
    spread = spread_matrix(groups, width, cpg, i * (width // cpg)).astype(bf16)
    return lax.dot_general(
        spec, spread, (((1,), (1,)), ((), ())), preferred_element_type=f32
    )


def own_kernel(
    cpg, width, here_ref, back_ref, p_ref, gc_ref, decay_ref, weight_ref, long_ref,
    near_ref, nearb_ref, taps_ref, corr_ref,
):
    rows, tile = p_ref.shape
    groups = long_ref.shape[1]
    corr_ref[...] = jnp.zeros_like(corr_ref)

    def body(i, at):
        spread = spread_matrix(groups, width, cpg, i * (width // cpg)).astype(bf16)
        head = modal_rows(weight_ref[:, at], decay_ref[:, at], rows, False)
        head = head + mm(long_ref[...], spread)
        head_spec = mm(here_ref[...], head.astype(bf16))
        own = mm(here_ref[...], p_ref[:, at])
        cur = mm(here_ref[...], gc_ref[:, at])
        near_ref[:, at] = mm(back_ref[...], times(own, head_spec, rows)).astype(bf16)
        nearb_ref[:, at] = mm(back_ref[...], times_conj(cur, head_spec, rows)).astype(bf16)
        corr_ref[...] += group_total(times_conj(cur, own, rows), groups, width, cpg, i)

    pieces(tile, width, body)
    taps_ref[...] = mm(back_ref[...], corr_ref[...].astype(bf16))


def last_kernel(
    cpg, width, taps, scale, here_ref, before_ref, back_ref, prev_ref, next_ref, gc_ref,
    near_ref, nearb_ref, qf_ref, kf_ref, vf_ref, g_ref, state_ref, decay_ref, weight_ref,
    long_ref, short_ref, tapsin_ref,
    lay_ref, gq_ref, gk_ref, gv_ref, head_ref, tail_ref, taps_ref, corr_ref, edge_ref,
):
    rows, tile = prev_ref.shape
    groups = long_ref.shape[1]
    corr_ref[...] = jnp.zeros_like(corr_ref)
    edge_ref[...] = mm(here_ref[...], long_ref[...]).astype(bf16)

    def body(i, at):
        spread = spread_matrix(groups, width, cpg, i * (width // cpg)).astype(bf16)
        short = short_ref[:, at]
        edge = mm(edge_ref[...], spread)
        prev = mm(before_ref[...], prev_ref[:, at])
        nxt = -mm(before_ref[...], next_ref[:, at])
        cur = mm(here_ref[...], gc_ref[:, at])
        decay, weight = decay_ref[:, at], weight_ref[:, at]
        poles = decay.shape[0]
        state = state_ref[:, at].astype(f32)
        corr_ref[...] += group_total(times_conj(cur, prev, rows), groups, width, cpg, i)
        conv = near_ref[:, at].astype(f32) + mm(back_ref[...], times(prev, edge, rows))
        conv = conv + modal_rows(
            weight * jnp.exp(-decay) * state[:poles], decay, rows, False
        )
        lay_ref[:, at] = (qf_ref[:, at].astype(f32) * conv).astype(bf16)
        grad = nearb_ref[:, at].astype(f32) + mm(back_ref[...], times_conj(nxt, edge, rows))
        grad = grad + modal_rows(weight * state[poles:], decay, rows, True)
        zero = jnp.zeros((SUB, width), f32)

        def finish(n, value, out_ref):
            value = value.astype(bf16)
            head_ref[n * SUB : (n + 1) * SUB, at] = value[:SUB]
            out = corr_rows(value.astype(f32), zero, short[n * SUB : n * SUB + taps])
            tail_ref[n * SUB : (n + 1) * SUB, at] = out[rows - SUB :]
            out_ref[:, at] = out.astype(bf16)

        finish(0, g_ref[:, at].astype(f32) * conv, gq_ref)
        finish(1, grad * vf_ref[:, at].astype(f32), gk_ref)
        finish(2, grad * kf_ref[:, at].astype(f32), gv_ref)

    pieces(tile, width, body)
    total = tapsin_ref[...] + mm(back_ref[...], corr_ref[...].astype(bf16))
    taps_ref[...] = total * scale


def edge_kernel(cpg, width, taps, rim_ref, tail_ref, short_ref, *refs):
    olds, outs = refs[:3], refs[3:]

    def body(i, at):
        short = short_ref[:, at]
        for n in range(3):
            part = short[n * SUB : n * SUB + taps]
            zero = jnp.zeros((SUB, width), f32)
            rim = rim_ref[n * SUB : (n + 1) * SUB, at].astype(f32)
            add = corr_rows(zero, rim, part)
            low = tail_ref[n * SUB : (n + 1) * SUB, at] + add
            outs[n][:, at] = jnp.concatenate(
                [olds[n][:SUB, at].astype(f32), low], axis=0
            ).astype(bf16)

    pieces(tail_ref.shape[1], width, body)


def params():
    return pltpu.CompilerParams(vmem_limit_bytes=VMEM_LIMIT)


def remote(ident):
    return pltpu.CompilerParams(
        vmem_limit_bytes=VMEM_LIMIT, collective_id=ident, has_side_effects=True
    )


def shards(query_proj, key_proj, value_proj, short_taps, long_taps, decay_rate, residues, grad_out):
    rows, chans = query_proj.shape
    owners = lax.axis_size("own")
    count = owners * lax.axis_size("ctx")
    tap_count = short_taps.shape[1]
    groups_own = short_taps.shape[2]
    groups = groups_own * owners
    cpg = chans // groups
    poles = decay_rate.shape[0]
    tile = groups_own * cpg
    steps = chans // tile
    width = 256
    shape = jax.ShapeDtypeStruct
    vmem = pl.BlockSpec(memory_space=pltpu.VMEM)

    rims = from_behind(
        jnp.concatenate([query_proj[-SUB:], key_proj[-SUB:], value_proj[-SUB:]], axis=0), AXES, 1
    )
    short_pad = jnp.pad(short_taps, ((0, 0), (0, SUB - tap_count), (0, 0))).reshape(
        3 * SUB, groups_own
    )
    weight_own = residues * jnp.sqrt(-jnp.expm1(-2.0 * decay_rate))
    short_all, decay_all = pl.pallas_call(
        functools.partial(gather_kernel, owners),
        in_specs=[vmem] * 2,
        out_specs=[vmem] * 2,
        out_shape=[
            shape((owners,) + short_pad.shape, f32), shape((owners,) + decay_rate.shape, f32)
        ],
        scratch_shapes=[pltpu.SemaphoreType.DMA((2, owners))] * 2,
        compiler_params=remote(0),
        name="gather",
    )(short_pad, decay_rate)
    here, before, back = odd_tables(rows)

    def cols(height, wide=tile):
        return pl.BlockSpec((height, wide), lambda i: (0, i))

    def owned(height, wide):
        return pl.BlockSpec((None, height, wide), lambda i: (i, 0, 0))

    def whole(height, wide):
        return pl.BlockSpec((height, wide), lambda i: (0, 0))

    big = shape((rows, chans), bf16)
    qf, kf, vf, product, conv, states, short_chan = pl.pallas_call(
        functools.partial(first_kernel, cpg, width, tap_count),
        grid=(steps,),
        in_specs=[cols(rows)] * 4 + [cols(3 * SUB), owned(3 * SUB, groups_own), owned(poles, tile)],
        out_specs=[cols(rows)] * 5 + [cols(2 * poles), cols(3 * SUB)],
        out_shape=[big] * 5
        + [shape((2 * poles, chans), bf16), shape((3 * SUB, chans), f32)],
        compiler_params=params(),
        cost_estimate=pl.CostEstimate(
            flops=100 * rows * chans, bytes_accessed=18 * rows * chans, transcendentals=0
        ),
        name="first",
    )(query_proj, key_proj, value_proj, grad_out, rims, short_all, decay_all)

    earlier = from_behind(product, AXES, 1)
    later = from_behind(conv, AXES, -1)

    part = chans // count
    sent = states.reshape(2 * poles, count, part).transpose(1, 0, 2)
    me = lax.axis_index("ctx") * owners + lax.axis_index("own")
    at_owner = lax.div(me * part, tile)
    rate = lax.dynamic_slice(
        decay_all, (at_owner, 0, me * part - at_owner * tile), (1, poles, part)
    )[0] * float(rows)
    slab = (count, 2 * poles, part)
    returned, weight_all, long_all = pl.pallas_call(
        functools.partial(exchange_kernel, owners, count),
        in_specs=[vmem] * 4,
        out_specs=[vmem] * 3,
        out_shape=[
            shape(slab, bf16),
            shape((owners,) + weight_own.shape, f32),
            shape((owners,) + long_taps.shape, bf16),
        ],
        scratch_shapes=[
            pltpu.VMEM(slab, bf16), pltpu.VMEM(slab, f32), pltpu.VMEM(slab, bf16),
            pltpu.SemaphoreType.DMA((2, count)), pltpu.SemaphoreType.DMA((2, count)),
            pltpu.SemaphoreType.DMA((2, owners)), pltpu.SemaphoreType.DMA((2, owners)),
        ],
        compiler_params=remote(1),
        name="exchange",
    )(sent, rate, weight_own, long_taps.astype(bf16))
    state_in = returned.transpose(1, 0, 2).reshape(2 * poles, chans)

    near, near_back, taps_own = pl.pallas_call(
        functools.partial(own_kernel, cpg, width),
        grid=(steps,),
        in_specs=[
            whole(2 * rows, rows), whole(rows, 2 * rows), cols(rows), cols(rows),
            owned(poles, tile), owned(poles, tile), owned(long_taps.shape[0], groups_own),
        ],
        out_specs=[cols(rows), cols(rows), cols(rows, groups_own)],
        out_shape=[big, big, shape((rows, groups), f32)],
        scratch_shapes=[pltpu.VMEM((2 * rows, groups_own), f32)],
        compiler_params=params(),
        cost_estimate=pl.CostEstimate(
            flops=14 * rows * rows * chans, bytes_accessed=8 * rows * chans, transcendentals=0
        ),
        name="own",
    )(here, back, product, conv, decay_all, weight_all, long_all)

    scale = 1.0 / math.sqrt(rows * count * cpg)
    layer_out, gq, gk, gv, heads, tails, taps_part = pl.pallas_call(
        functools.partial(last_kernel, cpg, width, tap_count, scale),
        grid=(steps,),
        in_specs=[whole(2 * rows, rows), whole(2 * rows, rows), whole(rows, 2 * rows)]
        + [cols(rows)] * 9
        + [
            cols(2 * poles), owned(poles, tile), owned(poles, tile),
            owned(long_taps.shape[0], groups_own), cols(3 * SUB), cols(rows, groups_own),
        ],
        out_specs=[cols(rows)] * 4 + [cols(3 * SUB), cols(3 * SUB), cols(rows, groups_own)],
        out_shape=[big] * 4
        + [
            shape((3 * SUB, chans), bf16), shape((3 * SUB, chans), f32),
            shape((rows, groups), f32),
        ],
        scratch_shapes=[
            pltpu.VMEM((2 * rows, groups_own), f32), pltpu.VMEM((2 * rows, groups_own), bf16)
        ],
        compiler_params=params(),
        cost_estimate=pl.CostEstimate(
            flops=16 * rows * rows * chans, bytes_accessed=26 * rows * chans, transcendentals=0
        ),
        name="last",
    )(
        here, before, back, earlier, later, conv, near, near_back, qf, kf, vf, grad_out,
        state_in, decay_all, weight_all, long_all, short_chan, taps_own,
    )

    rim_after = from_behind(heads, AXES, -1)
    bottom = pl.BlockSpec((2 * SUB, tile), lambda i: (rows // (2 * SUB) - 1, i))
    gq, gk, gv = pl.pallas_call(
        functools.partial(edge_kernel, cpg, width, tap_count),
        grid=(steps,),
        in_specs=[cols(3 * SUB)] * 3 + [bottom] * 3,
        out_specs=[bottom] * 3,
        out_shape=[big] * 3,
        input_output_aliases={3: 0, 4: 1, 5: 2},
        compiler_params=params(),
        name="edge",
    )(rim_after, tails, short_chan, gq, gk, gv)

    ctxs = count // owners
    high = rows // ctxs
    shares = taps_part.reshape(ctxs, high, owners, groups_own).transpose(0, 2, 1, 3)
    grad_taps = pl.pallas_call(
        functools.partial(reduce_kernel, owners, count),
        in_specs=[vmem],
        out_specs=vmem,
        out_shape=shape((ctxs, high, groups_own), f32),
        scratch_shapes=[
            pltpu.VMEM((count, high, groups_own), f32),
            pltpu.SemaphoreType.DMA((count,)), pltpu.SemaphoreType.DMA((count,)),
            pltpu.SemaphoreType.DMA((ctxs,)), pltpu.SemaphoreType.DMA((ctxs,)),
        ],
        compiler_params=remote(2),
        name="reduce",
    )(shares.reshape(count, high, groups_own)).reshape(rows, groups_own)
    return (layer_out, gq, gk, gv, grad_taps)


def solution(mesh):
    block = P(AXES, None)
    return jax.shard_map(
        shards,
        mesh=mesh,
        in_specs=(
            block, block, block, P(None, None, "own"), P(None, "own"), P(None, "own"),
            P(None, "own"), block,
        ),
        out_specs=(block, block, block, block, P(None, "own")),
        check_vma=False,
    )
```

```python
import functools
import math

import jax
import jax.numpy as jnp
from jax import lax
from jax.experimental import pallas as pl
from jax.experimental.pallas import tpu as pltpu
from jax.sharding import PartitionSpec as P

AXES = ("ctx", "own")
SUB = 8
LAST_INPUTS = 18
f32, bf16 = jnp.float32, jnp.bfloat16
VMEM_LIMIT = 48 * 1024 * 1024


def from_behind(value, axis, steps):
    count = lax.axis_size(axis)
    leading, last = (max(0, -steps), min(count, count - steps))
    return lax.ppermute(value, axis, [(source, source + steps) for source in range(leading, last)])


def mm(a, b):
    return jnp.dot(a, b, preferred_element_type=f32)


def odd_tables(rows):
    odd = 2 * jnp.arange(rows, dtype=jnp.int32)[:, None] + 1
    place = jnp.arange(rows, dtype=jnp.int32)[None, :]

    def matrix(at):
        angle = ((odd * at) % (4 * rows)).astype(f32) * (math.pi / (2 * rows))
        return jnp.concatenate([jnp.cos(angle), -jnp.sin(angle)], axis=0)

    here, before = matrix(place), matrix(place + 3 * rows)
    back = here.T / rows
    return here.astype(bf16), before.astype(bf16), back.astype(bf16)


def spread_matrix(groups, width, cpg, first):
    row = lax.broadcasted_iota(jnp.int32, (groups, width), 0)
    col = lax.broadcasted_iota(jnp.int32, (groups, width), 1)
    start = (row - first) * cpg
    return jnp.logical_and(col >= start, col < start + cpg)


def conv_rows(rim, main, taps):
    rows = main.shape[0]
    joined = jnp.concatenate([rim, main], axis=0)
    total = taps[0:1] * main
    for j in range(1, taps.shape[0]):
        total = total + taps[j : j + 1] * pltpu.roll(joined, j, 0)[SUB:]
    return total


def corr_rows(main, rim, taps):
    rows = main.shape[0]
    joined = jnp.concatenate([main, rim], axis=0)
    total = taps[0:1] * main
    for j in range(1, taps.shape[0]):
        total = total + taps[j : j + 1] * pltpu.roll(joined, rows + SUB - j, 0)[:rows]
    return total


def modal_rows(coeff, decay, rows, reverse):
    poles, width = decay.shape
    step = lax.broadcasted_iota(jnp.int32, (SUB, width), 0).astype(f32)
    lag = (SUB - step) if reverse else step
    hop = jnp.exp(-float(SUB) * decay)
    now = [coeff[r : r + 1] * jnp.exp(-decay[r : r + 1] * lag) for r in range(poles)]
    hops = [jnp.broadcast_to(hop[r : r + 1], (SUB, width)) for r in range(poles)]
    parts = []
    for k in range(rows // SUB):
        total = now[0]
        for r in range(1, poles):
            total = total + now[r]
        parts.append(total)
        if k + 1 < rows // SUB:
            now = [a * b for a, b in zip(now, hops)]
    if reverse:
        parts = parts[::-1]
    return jnp.concatenate(parts, axis=0)


def block_states(x, decay, reverse):
    poles, width = decay.shape
    rows = x.shape[0]
    step = lax.broadcasted_iota(jnp.int32, (SUB, width), 0).astype(f32)
    lag = step if reverse else (SUB - 1 - step)
    hop = jnp.exp(-float(SUB) * decay)
    order = list(range(rows // SUB))
    if reverse:
        order = order[::-1]
    states = []
    for r in range(poles):
        one = jnp.broadcast_to(hop[r : r + 1], (SUB, width))
        total = x[order[0] * SUB : (order[0] + 1) * SUB]
        for k in order[1:]:
            total = total * one + x[k * SUB : (k + 1) * SUB]
        states.append(
            jnp.sum(total * jnp.exp(-decay[r : r + 1] * lag), axis=0, keepdims=True)
        )
    return jnp.concatenate(states, axis=0)


def pieces(tile, width, body):
    def step(i, carry):
        body(i, pl.ds(pl.multiple_of(i * width, width), width))
        return carry

    lax.fori_loop(0, tile // width, step, 0)


def short_of(short_ref, groups, width, cpg, i):
    spread = spread_matrix(groups, width, cpg, i * (width // cpg)).astype(bf16)
    value = short_ref[...]
    count = value.shape[0]
    high = value.astype(bf16).astype(f32)
    both = mm(jnp.concatenate([high, value - high], axis=0).astype(bf16), spread)
    return both[:count] + both[count:]


def device_of(flat, owners):
    return (lax.div(flat, owners), lax.rem(flat, owners))


def put(src, dst, send, recv, device):
    return pltpu.make_async_remote_copy(
        src_ref=src,
        dst_ref=dst,
        send_sem=send,
        recv_sem=recv,
        device_id=device,
        device_id_type=pl.DeviceIdType.MESH,
    )


def loop(count, body):
    def step(k, carry):
        body(k)
        return carry

    lax.fori_loop(1, count, step, 0)


def greet(count, device):
    barrier = pltpu.get_barrier_semaphore()
    loop(
        count,
        lambda k: pl.semaphore_signal(
            barrier, inc=1, device_id=device(k), device_id_type=pl.DeviceIdType.MESH
        ),
    )
    pl.semaphore_wait(barrier, count - 1)


def gather_kernel(owners, *refs):
    number = (len(refs) - 2) // 2
    pairs = list(zip(refs[:number], refs[number : 2 * number]))
    send, recv = refs[2 * number :]
    ctx, own = lax.axis_index("ctx"), lax.axis_index("own")

    def device(k):
        return (ctx, lax.rem(own + k, owners))

    greet(owners, device)

    def copies(k):
        return [
            put(src, dst.at[own], send.at[n, k], recv.at[n, k], device(k))
            for n, (src, dst) in enumerate(pairs)
        ]

    loop(owners, lambda k: [c.start() for c in copies(k)] and None)
    for src, dst in pairs:
        dst[own] = src[...]
    loop(owners, lambda k: [c.wait() for c in copies(k)] and None)


def exchange_kernel(
    owners, count, st_ref, rate_ref, ret_ref, got, work, scanned, send, recv,
):
    ctx, own = lax.axis_index("ctx"), lax.axis_index("own")
    me = ctx * owners + own
    poles = rate_ref.shape[0]

    def device(k):
        return device_of(lax.rem(me + k, count), owners)

    greet(count, device)

    def out_copy(k):
        to = lax.rem(me + k, count)
        return put(st_ref.at[to], got.at[me], send.at[0, k], recv.at[0, k], device(k))

    def back_copy(k):
        to = lax.rem(me + k, count)
        return put(scanned.at[to], ret_ref.at[me], send.at[1, k], recv.at[1, k], device(k))

    loop(count, lambda k: out_copy(k).start())
    got[me] = st_ref[me]
    loop(count, lambda k: out_copy(k).wait())
    keep = jnp.exp(-rate_ref[...])

    def step(k, carry):
        ahead, behind = carry
        at = count - 1 - k
        work[k, :poles] = ahead
        work[at, poles:] = behind
        return (
            keep * ahead + got[k].astype(f32)[:poles],
            keep * behind + got[at].astype(f32)[poles:],
        )

    zero = jnp.zeros(keep.shape, f32)
    lax.fori_loop(0, count, step, (zero, zero))
    scanned[...] = work[...].astype(bf16)
    loop(count, lambda k: back_copy(k).start())
    ret_ref[me] = scanned[me]
    loop(count, lambda k: back_copy(k).wait())


def reduce_kernel(owners, count, part_ref, out_ref, got, send, recv, asend, arecv):
    ctx, own = lax.axis_index("ctx"), lax.axis_index("own")
    me = ctx * owners + own
    ctxs = count // owners

    def device(k):
        return device_of(lax.rem(me + k, count), owners)

    greet(count, device)

    def out_copy(k):
        to = lax.rem(me + k, count)
        return put(part_ref.at[to], got.at[me], send.at[k], recv.at[k], device(k))

    def all_copy(k):
        return put(
            out_ref.at[ctx], out_ref.at[ctx], asend.at[k], arecv.at[k],
            (lax.rem(ctx + k, ctxs), own),
        )

    loop(count, lambda k: out_copy(k).start())
    got[me] = part_ref[me]
    loop(count, lambda k: out_copy(k).wait())
    out_ref[ctx] = jnp.sum(got[...], axis=0)
    loop(ctxs, lambda k: all_copy(k).start())
    loop(ctxs, lambda k: all_copy(k).wait())


def first_kernel(
    cpg, width, taps, q_ref, k_ref, v_ref, g_ref, rim_ref, short_ref, decay_ref,
    qf_ref, kf_ref, vf_ref, p_ref, gc_ref, st_ref, sc_ref,
):
    groups = short_ref.shape[1]

    def body(i, at):
        short = short_of(short_ref, groups, width, cpg, i)
        sc_ref[:, at] = short
        rim = rim_ref[:, at].astype(f32)

        def feat(n, ref):
            out = conv_rows(
                rim[n * SUB : (n + 1) * SUB],
                ref[:, at].astype(f32),
                short[n * SUB : n * SUB + taps],
            )
            return out.astype(bf16)

        qf, kf, vf = feat(0, q_ref), feat(1, k_ref), feat(2, v_ref)
        qf_ref[:, at] = qf
        kf_ref[:, at] = kf
        vf_ref[:, at] = vf
        product = (kf.astype(f32) * vf.astype(f32)).astype(bf16)
        p_ref[:, at] = product
        conv = (g_ref[:, at].astype(f32) * qf.astype(f32)).astype(bf16)
        gc_ref[:, at] = conv
        decay = decay_ref[:, at]
        poles = decay.shape[0]
        st_ref[:, at] = jnp.concatenate(
            [
                block_states(product.astype(f32), decay, False),
                block_states(conv.astype(f32), decay, True),
            ],
            axis=0,
        ).astype(bf16)

    pieces(q_ref.shape[1], width, body)


def times(a, b, rows):
    ar, ai, br, bi = a[:rows], a[rows:], b[:rows], b[rows:]
    return jnp.concatenate([ar * br - ai * bi, ar * bi + ai * br], axis=0).astype(bf16)


def times_conj(a, b, rows):
    ar, ai, br, bi = a[:rows], a[rows:], b[:rows], b[rows:]
    return jnp.concatenate([ar * br + ai * bi, ai * br - ar * bi], axis=0).astype(bf16)


def group_total(spec, groups, width, cpg, i):
    spread = spread_matrix(groups, width, cpg, i * (width // cpg)).astype(bf16)
    return lax.dot_general(
        spec, spread, (((1,), (1,)), ((), ())), preferred_element_type=f32
    )


def own_kernel(
    cpg, width, here_ref, back_ref, p_ref, gc_ref, decay_ref, weight_ref, long_ref,
    near_ref, nearb_ref, taps_ref, corr_ref,
):
    rows, tile = p_ref.shape
    groups = long_ref.shape[1]
    corr_ref[...] = jnp.zeros_like(corr_ref)

    def body(i, at):
        spread = spread_matrix(groups, width, cpg, i * (width // cpg)).astype(bf16)
        head = modal_rows(weight_ref[:, at], decay_ref[:, at], rows, False)
        head = head + mm(long_ref[...], spread)
        head_spec = mm(here_ref[...], head.astype(bf16))
        own = mm(here_ref[...], p_ref[:, at])
        cur = mm(here_ref[...], gc_ref[:, at])
        near_ref[:, at] = mm(back_ref[...], times(own, head_spec, rows)).astype(bf16)
        nearb_ref[:, at] = mm(back_ref[...], times_conj(cur, head_spec, rows)).astype(bf16)
        corr_ref[...] += group_total(times_conj(cur, own, rows), groups, width, cpg, i)

    pieces(tile, width, body)
    taps_ref[...] = mm(back_ref[...], corr_ref[...].astype(bf16))


def last_kernel(
    cpg, width, taps, scale, here_ref, before_ref, back_ref, prev_ref, next_ref, gc_ref,
    near_ref, nearb_ref, qf_ref, kf_ref, vf_ref, g_ref, state_ref, decay_ref, weight_ref,
    long_ref, short_ref, tapsin_ref,
    lay_ref, gq_ref, gk_ref, gv_ref, head_ref, tail_ref, taps_ref, corr_ref, edge_ref,
):
    rows, tile = prev_ref.shape
    groups = long_ref.shape[1]
    corr_ref[...] = jnp.zeros_like(corr_ref)
    edge_ref[...] = mm(here_ref[...], long_ref[...]).astype(bf16)

    def body(i, at):
        spread = spread_matrix(groups, width, cpg, i * (width // cpg)).astype(bf16)
        short = short_ref[:, at]
        edge = mm(edge_ref[...], spread)
        prev = mm(before_ref[...], prev_ref[:, at])
        nxt = -mm(before_ref[...], next_ref[:, at])
        cur = mm(here_ref[...], gc_ref[:, at])
        decay, weight = decay_ref[:, at], weight_ref[:, at]
        poles = decay.shape[0]
        state = state_ref[:, at].astype(f32)
        corr_ref[...] += group_total(times_conj(cur, prev, rows), groups, width, cpg, i)
        conv = near_ref[:, at].astype(f32) + mm(back_ref[...], times(prev, edge, rows))
        conv = conv + modal_rows(
            weight * jnp.exp(-decay) * state[:poles], decay, rows, False
        )
        lay_ref[:, at] = (qf_ref[:, at].astype(f32) * conv).astype(bf16)
        grad = nearb_ref[:, at].astype(f32) + mm(back_ref[...], times_conj(nxt, edge, rows))
        grad = grad + modal_rows(weight * state[poles:], decay, rows, True)
        zero = jnp.zeros((SUB, width), f32)

        def finish(n, value, out_ref):
            value = value.astype(bf16)
            head_ref[n * SUB : (n + 1) * SUB, at] = value[:SUB]
            out = corr_rows(value.astype(f32), zero, short[n * SUB : n * SUB + taps])
            tail_ref[n * SUB : (n + 1) * SUB, at] = out[rows - SUB :]
            out_ref[:, at] = out.astype(bf16)

        finish(0, g_ref[:, at].astype(f32) * conv, gq_ref)
        finish(1, grad * vf_ref[:, at].astype(f32), gk_ref)
        finish(2, grad * kf_ref[:, at].astype(f32), gv_ref)

    pieces(tile, width, body)
    total = tapsin_ref[...] + mm(back_ref[...], corr_ref[...].astype(bf16))
    taps_ref[...] = total * scale


def last_again(cpg, width, taps, scale, *refs):
    last_kernel(cpg, width, taps, scale, *refs[:LAST_INPUTS], *refs[LAST_INPUTS + 4 :])


def edge_kernel(cpg, width, taps, rim_ref, tail_ref, short_ref, *refs):
    olds, outs = refs[:3], refs[3:]

    def body(i, at):
        short = short_ref[:, at]
        for n in range(3):
            part = short[n * SUB : n * SUB + taps]
            zero = jnp.zeros((SUB, width), f32)
            rim = rim_ref[n * SUB : (n + 1) * SUB, at].astype(f32)
            add = corr_rows(zero, rim, part)
            low = tail_ref[n * SUB : (n + 1) * SUB, at] + add
            outs[n][:, at] = jnp.concatenate(
                [olds[n][:SUB, at].astype(f32), low], axis=0
            ).astype(bf16)

    pieces(tail_ref.shape[1], width, body)


def params():
    return pltpu.CompilerParams(vmem_limit_bytes=VMEM_LIMIT)


def remote(ident):
    return pltpu.CompilerParams(
        vmem_limit_bytes=VMEM_LIMIT, collective_id=ident, has_side_effects=True
    )


def shards(query_proj, key_proj, value_proj, short_taps, long_taps, decay_rate, residues, grad_out):
    rows, chans = query_proj.shape
    owners = lax.axis_size("own")
    count = owners * lax.axis_size("ctx")
    tap_count = short_taps.shape[1]
    groups_own = short_taps.shape[2]
    groups = groups_own * owners
    cpg = chans // groups
    poles = decay_rate.shape[0]
    tile = groups_own * cpg
    steps = chans // tile
    width = 256
    shape = jax.ShapeDtypeStruct
    vmem = pl.BlockSpec(memory_space=pltpu.VMEM)

    rims = from_behind(
        jnp.concatenate([query_proj[-SUB:], key_proj[-SUB:], value_proj[-SUB:]], axis=0), AXES, 1
    )
    short_pad = jnp.pad(short_taps, ((0, 0), (0, SUB - tap_count), (0, 0))).reshape(
        3 * SUB, groups_own
    )
    weight_own = residues * jnp.sqrt(-jnp.expm1(-2.0 * decay_rate))
    mine = (short_pad, decay_rate, weight_own, long_taps.astype(bf16))
    short_all, decay_all, weight_all, long_all = pl.pallas_call(
        functools.partial(gather_kernel, owners),
        in_specs=[vmem] * 4,
        out_specs=[vmem] * 4,
        out_shape=[shape((owners,) + x.shape, x.dtype) for x in mine],
        scratch_shapes=[pltpu.SemaphoreType.DMA((4, owners))] * 2,
        compiler_params=remote(0),
        name="gather",
    )(*mine)
    here, before, back = odd_tables(rows)

    cuts = 2 if steps % 2 == 0 else 1
    piece = steps // cuts
    part_chans = piece * tile

    def cols(height, wide=tile):
        return pl.BlockSpec((height, wide), lambda i: (0, i))

    def cut_cols(cut, height, wide=tile):
        return pl.BlockSpec((height, wide), lambda i: (0, cut * piece + i))

    def owned(cut, height, wide):
        return pl.BlockSpec((None, height, wide), lambda i: (cut * piece + i, 0, 0))

    def whole(height, wide):
        return pl.BlockSpec((height, wide), lambda i: (0, 0))

    big = shape((rows, chans), bf16)
    half = shape((rows, part_chans), bf16)
    firsts, halos = [], []
    for cut in range(cuts):
        made = pl.pallas_call(
            functools.partial(first_kernel, cpg, width, tap_count),
            grid=(piece,),
            in_specs=[cut_cols(cut, rows)] * 4
            + [
                cut_cols(cut, 3 * SUB), owned(cut, 3 * SUB, groups_own),
                owned(cut, poles, tile),
            ],
            out_specs=[cols(rows)] * 5 + [cols(2 * poles), cols(3 * SUB)],
            out_shape=[half] * 5
            + [shape((2 * poles, part_chans), bf16), shape((3 * SUB, part_chans), f32)],
            compiler_params=params(),
            cost_estimate=pl.CostEstimate(
                flops=6000 * rows * part_chans, bytes_accessed=18 * rows * part_chans,
                transcendentals=0,
            ),
            name="first",
        )(query_proj, key_proj, value_proj, grad_out, rims, short_all, decay_all)
        firsts.append(made)
        halos.append((from_behind(made[3], AXES, 1), from_behind(made[4], AXES, -1)))

    nears = []
    for cut in range(cuts):
        nears.append(
            pl.pallas_call(
                functools.partial(own_kernel, cpg, width),
                grid=(piece,),
                in_specs=[
                    whole(2 * rows, rows), whole(rows, 2 * rows), cols(rows), cols(rows),
                    owned(cut, poles, tile), owned(cut, poles, tile),
                    owned(cut, long_taps.shape[0], groups_own),
                ],
                out_specs=[cols(rows), cols(rows), cols(rows, groups_own)],
                out_shape=[half, half, shape((rows, piece * groups_own), f32)],
                scratch_shapes=[pltpu.VMEM((2 * rows, groups_own), f32)],
                compiler_params=params(),
                cost_estimate=pl.CostEstimate(
                    flops=90 * rows * rows * part_chans,
                    bytes_accessed=8 * rows * part_chans, transcendentals=0,
                ),
                name="own",
            )(here, back, firsts[cut][3], firsts[cut][4], decay_all, weight_all, long_all)
        )

    part = chans // count
    states = jnp.concatenate([made[5] for made in firsts], axis=1)
    short_chan = jnp.concatenate([made[6] for made in firsts], axis=1)
    sent = states.reshape(2 * poles, count, part).transpose(1, 0, 2)
    me = lax.axis_index("ctx") * owners + lax.axis_index("own")
    at_owner = lax.div(me * part, tile)
    rate = lax.dynamic_slice(
        decay_all, (at_owner, 0, me * part - at_owner * tile), (1, poles, part)
    )[0] * float(rows)
    sent, nears = lax.optimization_barrier((sent, nears))
    slab = (count, 2 * poles, part)
    returned = pl.pallas_call(
        functools.partial(exchange_kernel, owners, count),
        in_specs=[vmem] * 2,
        out_specs=vmem,
        out_shape=shape(slab, bf16),
        scratch_shapes=[
            pltpu.VMEM(slab, bf16), pltpu.VMEM(slab, f32), pltpu.VMEM(slab, bf16),
            pltpu.SemaphoreType.DMA((2, count)), pltpu.SemaphoreType.DMA((2, count)),
        ],
        compiler_params=remote(1),
        name="exchange",
    )(sent, rate)
    state_in = returned.transpose(1, 0, 2).reshape(2 * poles, chans)

    scale = 1.0 / math.sqrt(rows * count * cpg)
    results, small = (), []
    for cut in range(cuts):
        qf, kf, vf, _, conv, _, short_part = firsts[cut]
        near, near_back, taps_own = nears[cut]
        outs = pl.pallas_call(
            functools.partial(last_again if cut else last_kernel, cpg, width, tap_count, scale),
            grid=(piece,),
            in_specs=[whole(2 * rows, rows), whole(2 * rows, rows), whole(rows, 2 * rows)]
            + [cols(rows)] * 8
            + [
                cut_cols(cut, rows), cut_cols(cut, 2 * poles), owned(cut, poles, tile),
                owned(cut, poles, tile), owned(cut, long_taps.shape[0], groups_own),
                cols(3 * SUB), cols(rows, groups_own),
            ]
            + [pl.BlockSpec(memory_space=pl.ANY)] * len(results),
            out_specs=[cut_cols(cut, rows)] * 4
            + [cols(3 * SUB), cols(3 * SUB), cols(rows, groups_own)],
            out_shape=[big] * 4
            + [
                shape((3 * SUB, part_chans), bf16), shape((3 * SUB, part_chans), f32),
                shape((rows, piece * groups_own), f32),
            ],
            input_output_aliases={LAST_INPUTS + n: n for n in range(len(results))},
            scratch_shapes=[
                pltpu.VMEM((2 * rows, groups_own), f32),
                pltpu.VMEM((2 * rows, groups_own), bf16),
            ],
            compiler_params=params(),
            cost_estimate=pl.CostEstimate(
                flops=16 * rows * rows * part_chans, bytes_accessed=26 * rows * part_chans,
                transcendentals=0,
            ),
            name="last",
        )(
            here, before, back, *halos[cut], conv, near, near_back, qf, kf, vf, grad_out,
            state_in, decay_all, weight_all, long_all, short_part, taps_own, *results,
        )
        results = tuple(outs[:4])
        small.append(outs[4:])
    layer_out, gq, gk, gv = results
    heads, tails, taps_part = (jnp.concatenate(x, axis=1) for x in zip(*small))

    rim_after = from_behind(heads, AXES, -1)
    bottom = pl.BlockSpec((2 * SUB, tile), lambda i: (rows // (2 * SUB) - 1, i))
    gq, gk, gv = pl.pallas_call(
        functools.partial(edge_kernel, cpg, width, tap_count),
        grid=(steps,),
        in_specs=[cols(3 * SUB)] * 3 + [bottom] * 3,
        out_specs=[bottom] * 3,
        out_shape=[big] * 3,
        input_output_aliases={3: 0, 4: 1, 5: 2},
        compiler_params=params(),
        name="edge",
    )(rim_after, tails, short_chan, gq, gk, gv)

    ctxs = count // owners
    high = rows // ctxs
    shares = taps_part.reshape(ctxs, high, owners, groups_own).transpose(0, 2, 1, 3)
    grad_taps = pl.pallas_call(
        functools.partial(reduce_kernel, owners, count),
        in_specs=[vmem],
        out_specs=vmem,
        out_shape=shape((ctxs, high, groups_own), f32),
        scratch_shapes=[
            pltpu.VMEM((count, high, groups_own), f32),
            pltpu.SemaphoreType.DMA((count,)), pltpu.SemaphoreType.DMA((count,)),
            pltpu.SemaphoreType.DMA((ctxs,)), pltpu.SemaphoreType.DMA((ctxs,)),
        ],
        compiler_params=remote(2),
        name="reduce",
    )(shares.reshape(count, high, groups_own)).reshape(rows, groups_own)
    return (layer_out, gq, gk, gv, grad_taps)


def solution(mesh):
    block = P(AXES, None)
    return jax.shard_map(
        shards,
        mesh=mesh,
        in_specs=(
            block, block, block, P(None, None, "own"), P(None, "own"), P(None, "own"),
            P(None, "own"), block,
        ),
        out_specs=(block, block, block, block, P(None, "own")),
        check_vma=False,
    )
```
